512 devices in a mesh: sec: 32 (over x, y), term: 16 (over z, core).
Axes of the slice: x: 4, y: 8, z: 8, core: 2. Of those that a mesh axis runs over, the one named last changes fastest.
Arguments:
- vectors: bfloat16 [2, 32, 4, 256, 256], P(None, 'sec'), may hold values from -6 to 6
- left_ops: bfloat16 [48, 32, 256, 256], P('term', 'sec'), may hold values from -0.375 to 0.375
- right_ops: bfloat16 [48, 32, 256, 256], P('term', 'sec'), may hold values from -0.0546875 to 0.0546875
- offsets: int32 [48, 4], P('term'), may hold values from 0 to 31, as said below
Outputs:
- products: bfloat16 [2, 32, 4, 256, 256], P(None, 'sec', None, 'term')
- rayleigh: float32 [2, 2], replicated
The draws below stay inside these ranges and needn't reach their ends.
Inputs may be any that keep to these rules, and one draw needn't show every extreme that they name: Each term's 4 offsets are distinct, and every shift from 0 to 31 occurs for some term and pair.
All inputs are finite; a program needn't handle non-finite values.
Results may differ from the reference program's by a relative error of at most 0.015.
Values may be sent and summed in bfloat16 or wider, within the bound.
A program may use at most 64 MiB of HBM per device.

```python
import jax
import jax.numpy as jnp
from jax import lax

B = 256
P_SIZE = 4
S = 32
TERMS = 48


def draw_offsets(key, part):
    order = jax.random.permutation(key, S).astype(jnp.int32)
    first = jax.random.randint(jax.random.fold_in(key, 3), (), 0, S).astype(jnp.int32)
    positions = ((first + jnp.arange(TERMS * P_SIZE, dtype=jnp.int32)) % S).astype(jnp.int32)
    table = order[positions].reshape(TERMS, P_SIZE)
    row_order = jax.random.permutation(jax.random.fold_in(key, 5), TERMS).astype(jnp.int32)
    return table[row_order].astype(jnp.int32)


def block_scale(rng, extent, shards, low, high):
    loudness = 1.0
    for position, parts in shards:
        steps = jax.random.uniform(jax.random.fold_in(jax.random.fold_in(rng, 6), position), (parts,), jnp.float32, low / len(shards), high / len(shards))
        loudness = loudness * jnp.repeat(jnp.exp(steps), extent[position] // parts).reshape((-1,) + (1,) * (len(extent) - 1 - position))
    return loudness


def gaussian(own_key, shape, deviation, reach, split=(), kind=jnp.bfloat16):
    level = block_scale(own_key, shape, split, -0.22, 0.18) if split else 1.0
    result = jax.random.normal(own_key, shape, jnp.float32) * deviation * level
    return jnp.minimum(jnp.maximum(result, -reach), reach).astype(kind)


def setup_inputs(seed: int = 0) -> dict:
    arg_keys = jax.random.split(jax.random.key(seed), 5)
    vectors = gaussian(arg_keys[0], (2, S, P_SIZE, B, B), 1.0, 6.0, ((1, 32),))
    left_ops = gaussian(arg_keys[1], (TERMS, S, B, B), B ** -0.5, 0.375, ((0, 16), (1, 32)))
    right_ops = gaussian(arg_keys[2], (TERMS, S, B, B), (B * TERMS) ** -0.5, 0.0546875, ((0, 16), (1, 32)))
    offsets = draw_offsets(jax.random.fold_in(arg_keys[4], 71), 0)
    return {"vectors": vectors, "left_ops": left_ops, "right_ops": right_ops, "offsets": offsets}


def reference(vectors, left_ops, right_ops, offsets):
    sector_ids = jnp.arange(S, dtype=jnp.int32)
    right_sector = ((sector_ids[None, :, None] + offsets[:, None, :]) % S).astype(jnp.int32)
    wave = vectors.astype(jnp.float32)

    def one_term(running, operands):
        left_block, right_block, sector_table = operands
        inner_part = jnp.einsum('lab,ilpbc->ilpac', left_block.astype(jnp.float32), wave).astype(jnp.bfloat16)
        chosen = right_block[sector_table]
        added = jnp.einsum('ilpac,lpcd->ilpad', inner_part.astype(jnp.float32), chosen.astype(jnp.float32))
        return (running + added, None)
    start_value = jnp.zeros(vectors.shape, jnp.float32)
    products_full, _ = lax.scan(one_term, start_value, (left_ops, right_ops, right_sector))
    gram_matrix = jnp.einsum('ilpab,jlpab->ij', wave, products_full)
    squares = lax.optimization_barrier(jnp.sum(wave * wave, axis=(1, 2, 3, 4)))
    rayleigh = gram_matrix / jnp.sqrt(squares[:, None] * squares[None, :])
    return (products_full.astype(jnp.bfloat16), rayleigh)
```

```python
import functools

import jax
import jax.numpy as jnp
from jax import lax
from jax.experimental import pallas as pl
from jax.experimental.pallas import tpu as pltpu
from jax.sharding import PartitionSpec as P

MESH = pl.DeviceIdType.MESH
X = 4
C = 2
ORDER = (0, 3, 1, 2)


def kernel(Y, Z, off_ref, v_ref, l_ref, rt_ref, prod_ref, ray_ref,
           rg, lg, vg, inner, part, vcol, half, other, zsend, zgot, fin, fgot,
           gx, gk, gz, gy, send, recv):
    NI, PP, B, _ = v_ref.shape
    T = l_ref.shape[0]
    Q = B // X
    PH = PP // C
    sec, term = lax.axis_index("sec"), lax.axis_index("term")
    x, y = sec // Y, sec % Y
    z, k = term // C, term % C

    def at(dx=0, dy=0, dz=0, dk=0):
        return (((x + dx) % X) * Y + (y + dy) % Y, ((z + dz) % Z) * C + (k + dk) % C)

    barrier = pltpu.get_barrier_semaphore()
    peers = [at(dx=d) for d in range(1, X)] + [at(dy=d) for d in range(1, Y)]
    peers += [at(dz=d) for d in range(1, Z)] + [at(dk=1)]
    for peer in peers:
        pl.semaphore_signal(barrier, inc=1, device_id=peer, device_id_type=MESH)
    pl.semaphore_wait(barrier, len(peers))

    started = []

    def copy(src, dst, where):
        n = len(started)
        made = pltpu.make_async_remote_copy(
            src_ref=src, dst_ref=dst, send_sem=send.at[n], recv_sem=recv.at[n],
            device_id=where, device_id_type=MESH)
        made.start()
        started.append(made)
        return made

    rx = {d: copy(rt_ref.at[(x + d) % X], rg.at[0, (-d) % X], at(dx=d)) for d in (1, 3, 2)}
    rg[0, 0] = rt_ref[x]
    ring = {}

    def ring_send(d, j):
        spot = ORDER.index(j)
        for way in (1, -1):
            if 2 * d == Y and (spot < X // 2) != (way == 1):
                continue
            src = rg.at[(-way * (d - 1)) % Y, j]
            ring[d, j, way] = copy(src, rg.at[(-way * d) % Y, j], at(dy=way))

    def ring_pass(d, j):
        for way in (1, -1):
            if (d, j, way) in ring:
                ring[d, j, way].wait_recv()
        if 2 * d < Y:
            ring_send(d + 1, j)

    ring_send(1, 0)
    lx = {1: copy(l_ref, lg.at[3], at(dx=1)), -1: copy(l_ref, lg.at[1], at(dx=-1))}
    mine = pl.ds(k * PH, PH)
    vx = {}
    for first in (0, 1):
        for way in (1, -1):
            i = first if way == 1 else 1 - first
            vx[way, i] = copy(v_ref.at[i, mine], vg.at[(-way) % X, i, mine], at(dx=way))

    def make_inner(o):
        d = ORDER[o]

        def body(n, carry):
            t, p = n // PP, n % PP
            left = l_ref[t] if d == 0 else lg[d, t]
            for i in range(NI):
                v = v_ref[i, p] if d == 0 else vg[d, i, p]
                inner[o, t, p, i * B:(i + 1) * B] = jnp.dot(
                    left, v, preferred_element_type=jnp.float32).astype(jnp.bfloat16)
            return carry

        lax.fori_loop(0, T * PP, body, 0)

    def make_columns(o):
        d = ORDER[o]
        for q in range(X):
            @pl.when(x == q)
            def _():
                for i in range(NI):
                    for p in range(PP):
                        v = v_ref[i, p, :, q * Q:(q + 1) * Q] if d == 0 else vg[d, i, p, :, q * Q:(q + 1) * Q]
                        vcol[o, i, :, :, p * Q:(p + 1) * Q] = v.reshape(Z * C, B // (Z * C), Q)

    make_inner(0)
    for d in (1, 3, 2):
        rx[d].wait_recv()
        ring_send(1, (-d) % X)
    make_columns(0)

    def squares(n, carry):
        rows = pl.ds(pl.multiple_of(n * 16, 16), 16)
        out = []
        for i in range(NI):
            total = carry[i]
            for p in range(PP):
                v = v_ref[i, p, rows].astype(jnp.float32)
                total = total + v * v
            out.append(total)
        return tuple(out)

    zero = jnp.zeros((16, B), jnp.float32)
    square = lax.fori_loop(0, B // 16, squares, (zero,) * NI)

    ring_order = (0, 3, 1, 2) if X == 4 else range(X)
    for j in ring_order:
        ring_pass(1, j)

    hb = B // 2
    vcore, vfwd, lfwd = [], {}, {}
    lx[1].wait_recv()
    lfwd[1] = copy(lg.at[3, :, 0:hb], lg.at[2, :, 0:hb], at(dx=1))
    lx[-1].wait_recv()
    lfwd[-1] = copy(lg.at[1, :, hb:B], lg.at[2, :, hb:B], at(dx=-1))

    def arrived(way, i):
        vx[way, i].wait_recv()
        slot = (-way) % X
        if (way, i) in ((1, 0), (-1, 1)):
            vfwd[way] = copy(vg.at[slot, i, mine], vg.at[2, i, mine], at(dx=way))
        vcore.append(copy(vg.at[slot, i, mine], vg.at[slot, i, mine], at(dk=1)))

    for j in ring_order:
        if 2 * 2 <= Y:
            ring_pass(2, j)
    arrived(1, 0)
    arrived(-1, 1)
    if 2 * 3 <= Y:
        ring_pass(3, 0)
        ring_pass(3, 3)
    arrived(1, 1)
    arrived(-1, 0)
    if 2 * 3 <= Y:
        ring_pass(3, 1)
        ring_pass(3, 2)
    for made in vcore:
        made.wait_recv()
    make_inner(1)
    make_columns(1)
    make_inner(2)
    make_columns(2)
    if 2 * 4 <= Y:
        for j in ring_order:
            ring_pass(4, j)

    def outer(o):
        d = ORDER[o]
        for p in range(PP):
            total = None
            for t in range(T):
                off = off_ref[t, p]
                dy = off % Y
                dx = (d + off // Y + jnp.where(y + dy >= Y, 1, 0)) % X
                here = lax.dot_general(
                    inner[o, t, p], rg[dy, dx, t], (((1,), (1,)), ((), ())),
                    preferred_element_type=jnp.float32)
                total = here if total is None else total + here
            part[o, :, :, :, p * Q:(p + 1) * Q] = total.reshape(NI, Z * C, B // (Z * C), Q)

    swap, zcopy = {}, []

    def swap_send(o):
        for i in range(NI):
            for n in range(Z):
                half[o, i, n] = part[o, i, n * C + 1 - k].astype(jnp.bfloat16)
        swap[o] = copy(half.at[o], other.at[o], at(dk=1))

    def swap_add(o):
        swap[o].wait_recv()
        for i in range(NI):
            for n in range(Z):
                total = part[o, i, n * C + k] + other[o, i, n].astype(jnp.float32)
                zsend[n, o, i] = total.astype(jnp.bfloat16)

    def z_send(first):
        some = pl.ds(first, X // 2)
        for d in range(1, Z):
            zcopy.append(copy(zsend.at[(z + d) % Z, some], zgot.at[d - 1, some], at(dz=d)))

    def gram_add(o, carry):
        def body(n, carry):
            out = list(carry)
            for i in range(NI):
                v = vcol[o, i, n].astype(jnp.float32)
                for j in range(NI):
                    out[i * NI + j] = out[i * NI + j] + v * part[o, j, n]
            return tuple(out)

        return lax.fori_loop(0, Z * C, body, carry)

    gram = (jnp.zeros((B // (Z * C), PP * Q), jnp.float32),) * (NI * NI)
    outer(0)
    swap_send(0)
    outer(1)
    swap_send(1)
    swap_add(0)
    outer(2)
    swap_send(2)
    swap_add(1)
    z_send(0)
    gram = gram_add(0, gram)
    gram = gram_add(1, gram)
    lfwd[1].wait_recv()
    lfwd[-1].wait_recv()
    for way, i in ((1, 0), (-1, 1)):
        vfwd[way].wait_recv()
        vcore.append(copy(vg.at[2, i, mine], vg.at[2, i, mine], at(dk=1)))
    for made in vcore[-2:]:
        made.wait_recv()
    make_inner(3)
    outer(3)
    swap_send(3)
    make_columns(3)
    swap_add(2)
    gram = gram_add(2, gram)
    swap_add(3)
    z_send(X // 2)
    gram = gram_add(3, gram)

    rows = [jnp.sum(g, axis=0, keepdims=True) for g in gram]
    rows += [jnp.sum(s, axis=0, keepdims=True) * (1.0 / (Z * C)) for s in square]
    W = rows[0].shape[1] // 2
    rows = [r[:, :W] + r[:, W:] for r in rows]
    for n, r in enumerate(rows):
        gx[x, n:n + 1] = r
    for n in range(len(rows), 8):
        gx[x, n:n + 1] = jnp.zeros_like(rows[0])

    def spread(buf, me, size, name):
        return [copy(buf.at[me], buf.at[me], at(**{name: d})) for d in range(1, size)]

    def total(buf, copies, size):
        for made in copies:
            made.wait_recv()
        out = buf[0]
        for n in range(1, size):
            out = out + buf[n]
        return out

    got = total(gx, spread(gx, x, X, "dx"), X)
    gk[k] = got
    got = total(gk, spread(gk, k, C, "dk"), C)
    gy[y] = got
    ycopies = spread(gy, y, Y, "dy")

    for made in zcopy:
        made.wait_recv()
    for o in range(X):
        for i in range(NI):
            total_block = zsend[z, o, i].astype(jnp.float32)
            for d in range(Z - 1):
                total_block = total_block + zgot[d, o, i].astype(jnp.float32)
            fin[o, i] = total_block.astype(jnp.bfloat16)
    fcopy = [copy(fin.at[o], fgot.at[x], at(dx=ORDER[o])) for o in range(1, X)]
    fgot[x] = fin[0]
    gz[z] = total(gy, ycopies, Y)
    zcopies = spread(gz, z, Z, "dz")
    for made in fcopy:
        made.wait_recv()
    for q in range(X):
        for i in range(NI):
            for p in range(PP):
                prod_ref[i, p, :, q * Q:(q + 1) * Q] = fgot[q, i, :, p * Q:(p + 1) * Q]
    got = jnp.sum(total(gz, zcopies, Z), axis=1, keepdims=True)
    for i in range(NI):
        for j in range(NI):
            a = got[NI * NI + i:NI * NI + i + 1]
            b = got[NI * NI + j:NI * NI + j + 1]
            n = i * NI + j
            ray_ref[i:i + 1, j:j + 1] = got[n:n + 1] / jnp.sqrt(a * b)
    for made in started:
        made.wait_send()
    assert len(started) <= send.shape[0]


def local(Y, Z, vectors, left_ops, right_ops, offsets):
    NI, _, PP, B, _ = vectors.shape
    T = left_ops.shape[0]
    Q, R = B // X, B // (Z * C)
    turned = right_ops[:, 0].transpose(2, 0, 1).reshape(X, Q, T, B).transpose(0, 2, 1, 3)
    bf, f32 = jnp.bfloat16, jnp.float32
    vmem = pltpu.VMEM
    W = PP * Q
    whole = pl.BlockSpec(memory_space=pltpu.VMEM)
    copies = 96 if Y == 8 else 96
    products, rayleigh = pl.pallas_call(
        functools.partial(kernel, Y, Z),
        out_shape=(jax.ShapeDtypeStruct((NI, PP, R, B), bf), jax.ShapeDtypeStruct((NI, NI), f32)),
        in_specs=[pl.BlockSpec(memory_space=pltpu.SMEM), whole, whole, whole],
        out_specs=(whole, whole),
        scratch_shapes=[
            vmem((Y, X, T, Q, B), bf),
            vmem((X, T, B, B), bf),
            vmem((X, NI, PP, B, B), bf),
            vmem((X, T, PP, NI * B, B), bf),
            vmem((X, NI, Z * C, R, W), f32),
            vmem((X, NI, Z * C, R, W), bf),
            vmem((X, NI, Z, R, W), bf),
            vmem((X, NI, Z, R, W), bf),
            vmem((Z, X, NI, R, W), bf),
            vmem((Z - 1, X, NI, R, W), bf),
            vmem((X, NI, R, W), bf),
            vmem((X, NI, R, W), bf),
            vmem((X, 8, W // 2), f32),
            vmem((C, 8, W // 2), f32),
            vmem((Z, 8, W // 2), f32),
            vmem((Y, 8, W // 2), f32),
            pltpu.SemaphoreType.DMA((copies,)),
            pltpu.SemaphoreType.DMA((copies,)),
        ],
        compiler_params=pltpu.CompilerParams(
            collective_id=0, has_side_effects=True, vmem_limit_bytes=52 * 1024 * 1024),
    )(offsets, vectors[:, 0], left_ops[:, 0], turned)
    return products[:, None], rayleigh


def solution(mesh):
    sectors, terms = mesh.shape["sec"], mesh.shape["term"]
    in_specs = (
        P(None, "sec", None, None, None),
        P("term", "sec", None, None),
        P("term", "sec", None, None),
        P("term", None),
    )
    out_specs = (P(None, "sec", None, "term", None), P())
    return jax.shard_map(
        functools.partial(local, sectors // X, terms // C),
        mesh=mesh, in_specs=in_specs, out_specs=out_specs, check_vma=False)
```

```python
import functools

import jax
import jax.numpy as jnp
from jax import lax
from jax.experimental import pallas as pl
from jax.experimental.pallas import tpu as pltpu
from jax.sharding import PartitionSpec as P

MESH = pl.DeviceIdType.MESH
X = 4
C = 2
H = 1
ORDER = (0, 3, 1, 2)
GROUPS = 18
ARRIVALS = 95


def kernel(Y, Z, off_ref, v_hbm, l_hbm, r_hbm, prod_ref, ray_ref,
           v_ref, l_ref, r_ref, rt, g0, g1, g2, lg, vg, inner, part, vcol, half, other,
           zsend, zgot, fin, fgot, gx, gk, gz, gy, load, send, recv):
    NI, PP, B, _ = v_ref.shape
    T = l_ref.shape[0]
    Q = B // X
    HQ = Q // H
    ZC = Z * C
    R = B // ZC
    PH = PP // C
    sec, term = lax.axis_index("sec"), lax.axis_index("term")
    x, y = sec // Y, sec % Y
    z, k = term // C, term % C
    w = z % 2
    f32, bf = jnp.float32, jnp.bfloat16

    def at(dx=0, dy=0, dz=0, dk=0):
        return (((x + dx) % X) * Y + (y + dy) % Y, ((z + dz) % Z) * C + (k + dk) % C)

    loads = [pltpu.make_async_copy(a, b, load.at[n]) for n, (a, b) in enumerate(
        ((r_hbm, r_ref), (v_hbm, v_ref), (l_hbm, l_ref)))]
    for made in loads:
        made.start()
    barrier = pltpu.get_barrier_semaphore()
    peers = [at(dx=d) for d in range(1, X)] + [at(dy=d) for d in range(1, Y)]
    peers += [at(dz=d) for d in range(1, Z)] + [at(dk=1)]
    for peer in peers:
        pl.semaphore_signal(barrier, inc=1, device_id=peer, device_id_type=MESH)
    loads[0].wait()
    for t in range(T):
        turned = r_ref[t].T
        for q in range(X):
            rt[q, t] = turned[q * Q:(q + 1) * Q]
    pieces = (g0, g1, g2)
    where = tuple((t, pl.ds(0, Q)) for t in range(T))
    for c, (t, rows) in enumerate(where):
        pieces[c][0] = rt[x, t, rows]
    loads[1].wait()
    loads[2].wait()
    pl.semaphore_wait(barrier, len(peers))

    used = []
    groups = {}

    def group(name):
        return groups.setdefault(name, len(groups))

    def fresh():
        used.append(0)
        return recv.at[len(used) - 1]

    def copy(src, dst, to, sent, got=None):
        made = pltpu.make_async_remote_copy(
            src_ref=src, dst_ref=dst, send_sem=send.at[group(sent)],
            recv_sem=fresh() if got is None else got,
            device_id=to, device_id_type=MESH)
        made.start()
        return made

    def drain(ref, sem):
        pltpu.make_async_copy(ref, ref, sem).wait()

    ring = {}

    def ring_send(c, d, first, count):
        g = pieces[c]
        for way in (1, -1):
            if 2 * d == Y and (first < X // 2) != (way == 1):
                continue
            ring[c, d, way, first, count] = copy(
                g.at[pl.ds(((-way * (d - 1)) % Y) * X + first, count)],
                g.at[pl.ds(((-way * d) % Y) * X + first, count)], at(dy=way), ("ring", c, way))

    def ring_pass(c, d):
        if 2 * d > Y:
            return
        for first in (0, 2):
            for key, made in list(ring.items()):
                if key[:2] == (c, d) and first <= key[3] < first + 2:
                    made.wait_recv()
            if 2 * d < Y:
                ring_send(c, d + 1, first, 2)

    rx = {}
    for c, (t, rows) in enumerate(where):
        got = None if c == 0 else fresh()
        for d in (1, 3, 2):
            rx[c, d] = copy(
                rt.at[(x + d) % X, t, rows], pieces[c].at[(-d) % X], at(dx=d), ("rx", c), got)
        rx[c] = got
        ring_send(c, 1, 0, 1)

    vx, vfwd, vz, vk, lx, lfwd = {}, {}, {}, {}, {}, {}

    def v_at(slot, i, n, core=k):
        return vg.at[(slot * NI + i) * PP + core * PH + n]

    for first in (0, 1):
        for way in (1, -1):
            n = first if way == 1 else 1 - first
            vx[way, n] = copy(v_ref.at[w, k * PH + n], v_at((-way) % X, w, n), at(dx=way), "v")

    def left_send(t):
        for way in (1, -1):
            lx[way, t] = copy(l_ref.at[t], lg.at[((-way) % X) * T + t], at(dx=way), "l")

    def left_pass(t):
        hb = B // 2
        for way in (1, -1):
            lx[way, t].wait_recv()
            rows = pl.ds(0 if way == 1 else hb, hb)
            lfwd[way, t] = copy(lg.at[((-way) % X) * T + t, rows], lg.at[2 * T + t, rows], at(dx=way), "l")

    def v_core_copy(slot, i, m, n):
        if (slot, m) not in vk:
            vk[slot, m] = fresh()
        copy(v_at(slot, i, n), v_at(slot, i, n), at(dk=1), "v", vk[slot, m])

    def v_share(slot, n):
        vz[slot, n] = copy(v_at(slot, w, n), v_at(slot, w, n), at(dz=-1 if n == 0 else 1), "v")
        v_core_copy(slot, w, 0, n)

    def v_pass(way, n):
        vx[way, n].wait_recv()
        slot = (-way) % X
        if (way, n) in ((1, 0), (-1, 1)):
            vfwd[n] = copy(v_at(slot, w, n), v_at(2, w, n), at(dx=way), "v")
        v_share(slot, n)

    def v_core(slot, n):
        vz[slot, n].wait_recv()
        v_core_copy(slot, 1 - w, 1, n)

    def v_wait(slot):
        for m in range(2):
            drain(vg.at[pl.ds(slot * NI * PP, PH)], vk[slot, m])

    def make_inner(o, t):
        d = ORDER[o]

        def body(p, carry):
            left = l_ref[t] if d == 0 else lg[d * T + t]
            for i in range(NI):
                v = v_ref[i, p] if d == 0 else vg[(d * NI + i) * PP + p]
                inner[o, t, p, i * B:(i + 1) * B] = jnp.dot(
                    left, v, preferred_element_type=f32).astype(bf)
            return carry

        lax.fori_loop(0, PP, body, 0)

    def make_columns(o):
        d = ORDER[o]
        for q in range(X):
            @pl.when(x == q)
            def _():
                def body(i, carry):
                    for p in range(PP):
                        for h in range(H):
                            cols = slice(q * Q + h * HQ, q * Q + (h + 1) * HQ)
                            v = v_ref[i, p, :, cols] if d == 0 else vg[(d * NI + i) * PP + p, :, cols]
                            vcol[h, o, i, :, :, p * HQ:(p + 1) * HQ] = v.reshape(ZC, R, HQ)
                    return carry

                lax.fori_loop(0, NI, body, 0)

    def outer(c, o):
        d = ORDER[o]
        t = where[c][0]
        for p in range(PP):
            off = off_ref[t, p]
            dy = off % Y
            dx = (d + off // Y + jnp.where(y + dy >= Y, 1, 0)) % X
            total = lax.dot_general(
                inner[o, t, p], pieces[c][dy * X + dx], (((1,), (1,)), ((), ())),
                preferred_element_type=f32)
            cols = slice(p * HQ, (p + 1) * HQ)
            for h in range(H):
                here = total[:, h * HQ:(h + 1) * HQ].reshape(NI, ZC, R, HQ)
                if c == 0:
                    part[h, o, :, :, :, cols] = here
                else:
                    part[h, o, :, :, :, cols] += here

    swap = {}
    zsem = [fresh() for h in range(H)]
    fsem = [fresh() for h in range(H)]

    def swap_send(h, o):
        for i in range(NI):
            for n in range(Z):
                half[h, o, i, n] = part[h, o, i, n * C + 1 - k].astype(bf)
        swap[h, o] = copy(half.at[h, o], other.at[h, o], at(dk=1), "swap")

    def swap_add(h, o):
        swap[h, o].wait_recv()
        for i in range(NI):
            for n in range(Z):
                total = part[h, o, i, n * C + k] + other[h, o, i, n].astype(f32)
                zsend[h, o, n, i] = total.astype(bf)
        for dz in sorted(range(1, Z), key=lambda d: -min(d, Z - d)):
            copy(zsend.at[h, o, (z + dz) % Z], zgot.at[h, ((-dz) % Z) * X + o], at(dz=dz), ("z", h), zsem[h])

    def gram_add(h, o, carry):
        def body(n, carry):
            out = list(carry)
            for i in range(NI):
                v = vcol[h, o, i, n].astype(f32)
                for j in range(NI):
                    out[i * NI + j] = out[i * NI + j] + v * part[h, o, j, n]
            return tuple(out)

        return lax.fori_loop(0, ZC, body, carry)

    def finish(h):
        drain(zgot.at[h, pl.ds(X, X * (Z - 1))], zsem[h])
        for o in range(X):
            for i in range(NI):
                total = zsend[h, o, z, i].astype(f32)
                for dz in range(1, Z):
                    total = total + zgot[h, dz * X + o, i].astype(f32)
                fin[h, o, i] = total.astype(bf)
            if o:
                copy(fin.at[h, o], fgot.at[h, x], at(dx=ORDER[o]), ("f", h), fsem[h])
        fgot[h, x] = fin[h, 0]

    def spread(buf, me, size, name):
        got = fresh()
        for d in range(1, size):
            copy(buf.at[me], buf.at[me], at(**{name: d}), name, got)
        return got

    def collect(buf, size, got):
        drain(buf.at[pl.ds(0, size - 1)], got)
        return jnp.sum(buf[...], axis=0)

    left_send(0)
    make_inner(0, 0)
    for d in (1, 3, 2):
        rx[0, d].wait_recv()
        ring_send(0, 1, (-d) % X, 1)
    make_inner(0, 1)
    for c in range(1, T):
        drain(pieces[c].at[pl.ds(1, X - 1)], rx[c])
        ring_send(c, 1, 1, 1)
        ring_send(c, 1, 2, 2)
    make_inner(0, 2)
    ring_pass(0, 1)
    v_pass(1, 0)
    v_pass(-1, 1)
    left_send(1)
    left_send(2)
    ring_pass(1, 1)
    make_columns(0)
    v_pass(1, 1)
    v_pass(-1, 0)
    ring_pass(0, 2)

    def squares(n, carry):
        rows = pl.ds(pl.multiple_of(n * 16, 16), 16)
        out = []
        for i in range(NI):
            total = carry[i]
            for p in range(PP):
                v = v_ref[i, p, rows].astype(f32)
                total = total + v * v
            out.append(total)
        return tuple(out)

    square = lax.fori_loop(0, B // 16, squares, (jnp.zeros((16, B), f32),) * NI)
    left_pass(0)
    ring_pass(1, 2)
    for slot in (3, 1):
        v_core(slot, 0)
        v_core(slot, 1)
    for n in range(PH):
        vfwd[n].wait_recv()
        v_share(2, n)
    ring_pass(2, 1)
    v_wait(3)
    make_inner(1, 0)
    ring_pass(0, 3)
    left_pass(1)
    make_inner(1, 1)
    ring_pass(1, 3)
    left_pass(2)
    make_inner(1, 2)
    v_core(2, 0)
    v_core(2, 1)
    v_wait(1)
    make_inner(2, 0)
    ring_pass(2, 2)
    make_inner(2, 1)
    ring_pass(0, 4)
    make_inner(2, 2)
    outer(0, 0)
    outer(0, 1)
    outer(0, 2)
    ring_pass(2, 3)
    ring_pass(1, 4)
    outer(1, 0)
    outer(1, 1)
    outer(1, 2)
    v_wait(2)
    for t in range(T):
        for way in (1, -1):
            lfwd[way, t].wait_recv()
        make_inner(3, t)
    outer(0, 3)
    outer(1, 3)
    ring_pass(2, 4)
    for o in range(X):
        outer(2, o)
        swap_send(0, o)
        if o:
            swap_add(0, o - 1)
    swap_add(0, 3)
    for o in range(1, X):
        make_columns(o)
    gram = (jnp.zeros((R, PP * HQ), f32),) * (NI * NI)
    for h in range(H):
        for o in range(X):
            gram = gram_add(h, o, gram)

    rows = [jnp.sum(g, axis=0, keepdims=True) for g in gram]
    W = rows[0].shape[1]
    for s in square:
        s = jnp.sum(s, axis=0, keepdims=True) * (1.0 / ZC)
        rows.append(sum(s[:, n * W:(n + 1) * W] for n in range(1, B // W)) + s[:, :W])
    for n in range(8):
        gk[k, n:n + 1] = rows[n] if n < len(rows) else jnp.zeros_like(rows[0])
    got_k = spread(gk, k, C, "dk")
    gx[x] = collect(gk, C, got_k)
    got_x = spread(gx, x, X, "dx")
    gy[y] = collect(gx, X, got_x)
    got_y = spread(gy, y, Y, "dy")
    gz[z] = collect(gy, Y, got_y)
    got_z = spread(gz, z, Z, "dz")
    finish(0)
    for h in range(H):
        drain(fgot.at[h, pl.ds(0, X - 1)], fsem[h])
    for q in range(X):
        for i in range(NI):
            for p in range(PP):
                prod_ref[i, p, :, q * Q:(q + 1) * Q] = jnp.concatenate(
                    [fgot[h, q, i, :, p * HQ:(p + 1) * HQ] for h in range(H)], axis=1)
    got = jnp.sum(collect(gz, Z, got_z), axis=1, keepdims=True)
    for i in range(NI):
        for j in range(NI):
            a = got[NI * NI + i:NI * NI + i + 1]
            b = got[NI * NI + j:NI * NI + j + 1]
            n = i * NI + j
            ray_ref[i:i + 1, j:j + 1] = got[n:n + 1] / jnp.sqrt(a * b)

    for c in range(T):
        for way in (1, -1):
            drain(pieces[c].at[pl.ds(0, X * (Y // 2 - 1) + X // 2)], send.at[group(("ring", c, way))])
        drain(pieces[c].at[pl.ds(0, X - 1)], send.at[group(("rx", c))])
    drain(vg.at[pl.ds(0, 24)], send.at[group("v")])
    drain(lg.at[pl.ds(0, 3 * T)], send.at[group("l")])
    drain(half, send.at[group("swap")])
    for h in range(H):
        drain(zgot.at[h, pl.ds(X, X * (Z - 1))], send.at[group(("z", h))])
        drain(fgot.at[h, pl.ds(0, X - 1)], send.at[group(("f", h))])
    for buf, size, name in ((gk, C, "dk"), (gx, X, "dx"), (gy, Y, "dy"), (gz, Z, "dz")):
        drain(buf.at[pl.ds(0, size - 1)], send.at[group(name)])
    assert len(used) <= recv.shape[0] and len(groups) <= send.shape[0], (len(used), len(groups))


def local(Y, Z, vectors, left_ops, right_ops, offsets):
    NI, _, PP, B, _ = vectors.shape
    T = left_ops.shape[0]
    Q, ZC = B // X, Z * C
    R, HQ = B // ZC, Q // H
    bf, f32 = jnp.bfloat16, jnp.float32
    vmem, dma = pltpu.VMEM, pltpu.SemaphoreType.DMA
    W = PP * HQ
    whole = pl.BlockSpec(memory_space=pltpu.VMEM)
    hbm = pl.BlockSpec(memory_space=pl.ANY)
    products, rayleigh = pl.pallas_call(
        functools.partial(kernel, Y, Z),
        out_shape=(jax.ShapeDtypeStruct((NI, PP, R, B), bf), jax.ShapeDtypeStruct((NI, NI), f32)),
        in_specs=[pl.BlockSpec(memory_space=pltpu.SMEM), hbm, hbm, hbm],
        out_specs=(whole, whole),
        scratch_shapes=[
            vmem((NI, PP, B, B), bf),
            vmem((T, B, B), bf),
            vmem((T, B, B), bf),
            vmem((X, T, Q, B), bf),
            vmem((Y * X, Q, B), bf),
            vmem((Y * X, Q, B), bf),
            vmem((Y * X, Q, B), bf),
            vmem((X * T, B, B), bf),
            vmem((X * NI * PP, B, B), bf),
            vmem((X, T, PP, NI * B, B), bf),
            vmem((H, X, NI, ZC, R, W), f32),
            vmem((H, X, NI, ZC, R, W), bf),
            vmem((H, X, NI, Z, R, W), bf),
            vmem((H, X, NI, Z, R, W), bf),
            vmem((H, X, Z, NI, R, W), bf),
            vmem((H, X * Z, NI, R, W), bf),
            vmem((H, X, NI, R, W), bf),
            vmem((H, X, NI, R, W), bf),
            vmem((X, 8, W), f32),
            vmem((C, 8, W), f32),
            vmem((Z, 8, W), f32),
            vmem((Y, 8, W), f32),
            dma((3,)),
            dma((GROUPS,)),
            dma((ARRIVALS,)),
        ],
        compiler_params=pltpu.CompilerParams(
            collective_id=0, has_side_effects=True, vmem_limit_bytes=56 * 1024 * 1024),
    )(offsets, vectors[:, 0], left_ops[:, 0], right_ops[:, 0])
    return products[:, None], rayleigh


def solution(mesh):
    sectors, terms = mesh.shape["sec"], mesh.shape["term"]
    in_specs = (
        P(None, "sec", None, None, None),
        P("term", "sec", None, None),
        P("term", "sec", None, None),
        P("term", None),
    )
    out_specs = (P(None, "sec", None, "term", None), P())
    return jax.shard_map(
        functools.partial(local, sectors // X, terms // C),
        mesh=mesh, in_specs=in_specs, out_specs=out_specs, check_vma=False)
```

```python
import functools

import jax
import jax.numpy as jnp
from jax import lax
from jax.experimental import pallas as pl
from jax.experimental.pallas import tpu as pltpu
from jax.sharding import PartitionSpec as P

MESH = pl.DeviceIdType.MESH
X = 4
C = 2
H = 1
ORDER = (0, 3, 1, 2)
GROUPS = 18
ARRIVALS = 95


def kernel(Y, Z, off_ref, v_hbm, l_hbm, r_hbm, prod_ref, ray_ref,
           v_ref, l_ref, r_ref, rt, g0, g1, g2, lg, vg, inner, part, vcol, half, other,
           zsend, zgot, fin, fgot, gx, gk, gz, gy, load, send, recv):
    NI, PP, B, _ = v_ref.shape
    T = l_ref.shape[0]
    Q = B // X
    HQ = Q // H
    ZC = Z * C
    R = B // ZC
    PH = PP // C
    sec, term = lax.axis_index("sec"), lax.axis_index("term")
    x, y = sec // Y, sec % Y
    z, k = term // C, term % C
    w = z % 2
    f32, bf = jnp.float32, jnp.bfloat16

    def at(dx=0, dy=0, dz=0, dk=0):
        return (((x + dx) % X) * Y + (y + dy) % Y, ((z + dz) % Z) * C + (k + dk) % C)

    loads = [pltpu.make_async_copy(a, b, load.at[n]) for n, (a, b) in enumerate(
        ((r_hbm, r_ref), (v_hbm, v_ref), (l_hbm, l_ref)))]
    for made in loads:
        made.start()
    barrier = pltpu.get_barrier_semaphore()
    peers = [at(dx=d) for d in range(1, X)] + [at(dy=d) for d in range(1, Y)]
    peers += [at(dz=d) for d in range(1, Z)] + [at(dk=1)]
    for peer in peers:
        pl.semaphore_signal(barrier, inc=1, device_id=peer, device_id_type=MESH)
    loads[0].wait()
    for t in range(T):
        turned = r_ref[t].T
        for q in range(X):
            rt[q, t] = turned[q * Q:(q + 1) * Q]
    pieces = (g0, g1, g2)
    where = tuple((t, pl.ds(0, Q)) for t in range(T))
    for c, (t, rows) in enumerate(where):
        pieces[c][0] = rt[x, t, rows]
    loads[1].wait()
    loads[2].wait()
    pl.semaphore_wait(barrier, len(peers))

    used = []
    groups = {}

    def group(name):
        return groups.setdefault(name, len(groups))

    def fresh():
        used.append(0)
        return recv.at[len(used) - 1]

    def copy(src, dst, to, sent, got=None):
        made = pltpu.make_async_remote_copy(
            src_ref=src, dst_ref=dst, send_sem=send.at[group(sent)],
            recv_sem=fresh() if got is None else got,
            device_id=to, device_id_type=MESH)
        made.start()
        return made

    def drain(ref, sem):
        pltpu.make_async_copy(ref, ref, sem).wait()

    ring = {}

    def ring_send(c, d, first, count):
        g = pieces[c]
        for way in (1, -1):
            if 2 * d == Y and (first < X // 2) != (way == 1):
                continue
            ring[c, d, way, first, count] = copy(
                g.at[pl.ds(((-way * (d - 1)) % Y) * X + first, count)],
                g.at[pl.ds(((-way * d) % Y) * X + first, count)], at(dy=way), ("ring", c, way))

    def ring_pass(c, d):
        if 2 * d > Y:
            return
        for first in (0, 2):
            for key, made in list(ring.items()):
                if key[:2] == (c, d) and first <= key[3] < first + 2:
                    made.wait_recv()
            if 2 * d < Y:
                ring_send(c, d + 1, first, 2)

    rx = {}
    for c, (t, rows) in enumerate(where):
        got = None if c == 0 else fresh()
        for d in (1, 3, 2):
            rx[c, d] = copy(
                rt.at[(x + d) % X, t, rows], pieces[c].at[(-d) % X], at(dx=d), ("rx", c), got)
        rx[c] = got
        ring_send(c, 1, 0, 1)

    vx, vfwd, vz, vk, lx, lfwd = {}, {}, {}, {}, {}, {}

    def v_at(slot, i, n, core=k):
        return vg.at[(slot * NI + i) * PP + core * PH + n]

    for first in (0, 1):
        for way in (1, -1):
            n = first if way == 1 else 1 - first
            vx[way, n] = copy(v_ref.at[w, k * PH + n], v_at((-way) % X, w, n), at(dx=way), "v")

    def left_send(t):
        for way in (1, -1):
            lx[way, t] = copy(l_ref.at[t], lg.at[((-way) % X) * T + t], at(dx=way), "l")

    def left_pass(t):
        hb = B // 2
        for way in (1, -1):
            lx[way, t].wait_recv()
            rows = pl.ds(0 if way == 1 else hb, hb)
            lfwd[way, t] = copy(lg.at[((-way) % X) * T + t, rows], lg.at[2 * T + t, rows], at(dx=way), "l")

    def v_core_copy(slot, i, m, n):
        if (slot, m) not in vk:
            vk[slot, m] = fresh()
        copy(v_at(slot, i, n), v_at(slot, i, n), at(dk=1), "v", vk[slot, m])

    def v_share(slot, n):
        vz[slot, n] = copy(v_at(slot, w, n), v_at(slot, w, n), at(dz=-1 if n == 0 else 1), "v")
        v_core_copy(slot, w, 0, n)

    def v_pass(way, n):
        vx[way, n].wait_recv()
        slot = (-way) % X
        if (way, n) in ((1, 0), (-1, 1)):
            vfwd[n] = copy(v_at(slot, w, n), v_at(2, w, n), at(dx=way), "v")
        v_share(slot, n)

    def v_core(slot, n):
        vz[slot, n].wait_recv()
        v_core_copy(slot, 1 - w, 1, n)

    def v_wait(slot):
        for m in range(2):
            drain(vg.at[pl.ds(slot * NI * PP, PH)], vk[slot, m])

    def make_inner(o, t):
        d = ORDER[o]

        def body(p, carry):
            left = l_ref[t] if d == 0 else lg[d * T + t]
            for i in range(NI):
                v = v_ref[i, p] if d == 0 else vg[(d * NI + i) * PP + p]
                inner[o, t, p, i * B:(i + 1) * B] = jnp.dot(
                    left, v, preferred_element_type=f32).astype(bf)
            return carry

        lax.fori_loop(0, PP, body, 0)

    def make_columns(o):
        d = ORDER[o]
        for q in range(X):
            @pl.when(x == q)
            def _():
                def body(i, carry):
                    for p in range(PP):
                        for h in range(H):
                            cols = slice(q * Q + h * HQ, q * Q + (h + 1) * HQ)
                            v = v_ref[i, p, :, cols] if d == 0 else vg[(d * NI + i) * PP + p, :, cols]
                            vcol[h, o, i, :, :, p * HQ:(p + 1) * HQ] = v.reshape(ZC, R, HQ)
                    return carry

                lax.fori_loop(0, NI, body, 0)

    def outer(c, o):
        d = ORDER[o]
        t = where[c][0]
        for p in range(PP):
            off = off_ref[t, p]
            dy = off % Y
            dx = (d + off // Y + jnp.where(y + dy >= Y, 1, 0)) % X
            total = lax.dot_general(
                inner[o, t, p], pieces[c][dy * X + dx], (((1,), (1,)), ((), ())),
                preferred_element_type=f32)
            cols = slice(p * HQ, (p + 1) * HQ)
            for h in range(H):
                here = total[:, h * HQ:(h + 1) * HQ].reshape(NI, ZC, R, HQ)
                if c == 0:
                    part[h, o, :, :, :, cols] = here
                else:
                    part[h, o, :, :, :, cols] += here

    swap = {}
    zsem = [fresh() for h in range(H)]
    fsem = [fresh() for h in range(H)]

    def swap_send(h, o):
        for i in range(NI):
            for n in range(Z):
                half[h, o, i, n] = part[h, o, i, n * C + 1 - k].astype(bf)
        swap[h, o] = copy(half.at[h, o], other.at[h, o], at(dk=1), "swap")

    def swap_add(h, o):
        swap[h, o].wait_recv()
        for i in range(NI):
            for n in range(Z):
                total = part[h, o, i, n * C + k] + other[h, o, i, n].astype(f32)
                zsend[h, o, n, i] = total.astype(bf)
        for dz in sorted(range(1, Z), key=lambda d: -min(d, Z - d)):
            copy(zsend.at[h, o, (z + dz) % Z], zgot.at[h, ((-dz) % Z) * X + o], at(dz=dz), ("z", h), zsem[h])

    def gram_add(h, o, carry):
        def body(n, carry):
            out = list(carry)
            for i in range(NI):
                v = vcol[h, o, i, n].astype(f32)
                for j in range(NI):
                    out[i * NI + j] = out[i * NI + j] + v * part[h, o, j, n]
            return tuple(out)

        return lax.fori_loop(0, ZC, body, carry)

    def finish(h):
        drain(zgot.at[h, pl.ds(X, X * (Z - 1))], zsem[h])
        for o in range(X):
            for i in range(NI):
                total = zsend[h, o, z, i].astype(f32)
                for dz in range(1, Z):
                    total = total + zgot[h, dz * X + o, i].astype(f32)
                fin[h, o, i] = total.astype(bf)
            if o:
                copy(fin.at[h, o], fgot.at[h, x], at(dx=ORDER[o]), ("f", h), fsem[h])
        fgot[h, x] = fin[h, 0]

    def spread(buf, me, size, name):
        got = fresh()
        for d in range(1, size):
            copy(buf.at[me], buf.at[me], at(**{name: d}), name, got)
        return got

    def collect(buf, size, got):
        drain(buf.at[pl.ds(0, size - 1)], got)
        return jnp.sum(buf[...], axis=0)

    left_send(0)
    make_inner(0, 0)
    for d in (1, 3, 2):
        rx[0, d].wait_recv()
        ring_send(0, 1, (-d) % X, 1)
    make_inner(0, 1)
    for c in range(1, T):
        drain(pieces[c].at[pl.ds(1, X - 1)], rx[c])
        ring_send(c, 1, 1, 1)
        ring_send(c, 1, 2, 2)
    make_inner(0, 2)
    ring_pass(0, 1)
    v_pass(1, 0)
    v_pass(-1, 1)
    left_send(1)
    left_send(2)
    ring_pass(1, 1)
    make_columns(0)
    v_pass(1, 1)
    v_pass(-1, 0)
    ring_pass(0, 2)

    def squares(n, carry):
        rows = pl.ds(pl.multiple_of(n * 16, 16), 16)
        out = []
        for i in range(NI):
            total = carry[i]
            for p in range(PP):
                v = v_ref[i, p, rows].astype(f32)
                total = total + v * v
            out.append(total)
        return tuple(out)

    square = lax.fori_loop(0, B // 16, squares, (jnp.zeros((16, B), f32),) * NI)
    left_pass(0)
    ring_pass(1, 2)
    ring_pass(2, 1)
    for slot in (3, 1):
        v_core(slot, 0)
        v_core(slot, 1)
    v_wait(3)
    make_inner(1, 0)
    ring_pass(0, 3)
    for n in range(PH):
        vfwd[n].wait_recv()
        v_share(2, n)
    left_pass(1)
    make_inner(1, 1)
    ring_pass(1, 3)
    left_pass(2)
    make_inner(1, 2)
    ring_pass(2, 2)
    v_wait(1)
    make_inner(2, 0)
    v_core(2, 0)
    v_core(2, 1)
    make_inner(2, 1)
    ring_pass(0, 4)
    make_inner(2, 2)
    outer(0, 0)
    outer(0, 1)
    outer(0, 2)
    ring_pass(2, 3)
    ring_pass(1, 4)
    outer(1, 0)
    outer(1, 1)
    outer(1, 2)
    v_wait(2)
    for t in range(T):
        for way in (1, -1):
            lfwd[way, t].wait_recv()
        make_inner(3, t)
    outer(0, 3)
    outer(1, 3)
    ring_pass(2, 4)
    for o in range(X):
        outer(2, o)
        swap_send(0, o)
        if o:
            swap_add(0, o - 1)
    swap_add(0, 3)
    for o in range(1, X):
        make_columns(o)
    gram = (jnp.zeros((R, PP * HQ), f32),) * (NI * NI)
    for h in range(H):
        for o in range(X):
            gram = gram_add(h, o, gram)

    rows = [jnp.sum(g, axis=0, keepdims=True) for g in gram]
    W = rows[0].shape[1]
    for s in square:
        s = jnp.sum(s, axis=0, keepdims=True) * (1.0 / ZC)
        rows.append(sum(s[:, n * W:(n + 1) * W] for n in range(1, B // W)) + s[:, :W])
    for n in range(8):
        gk[k, n:n + 1] = rows[n] if n < len(rows) else jnp.zeros_like(rows[0])
    got_k = spread(gk, k, C, "dk")
    gx[x] = collect(gk, C, got_k)
    got_x = spread(gx, x, X, "dx")
    gy[y] = collect(gx, X, got_x)
    got_y = spread(gy, y, Y, "dy")
    gz[z] = collect(gy, Y, got_y)
    got_z = spread(gz, z, Z, "dz")
    finish(0)
    for h in range(H):
        drain(fgot.at[h, pl.ds(0, X - 1)], fsem[h])
    for q in range(X):
        for i in range(NI):
            for p in range(PP):
                prod_ref[i, p, :, q * Q:(q + 1) * Q] = jnp.concatenate(
                    [fgot[h, q, i, :, p * HQ:(p + 1) * HQ] for h in range(H)], axis=1)
    got = jnp.sum(collect(gz, Z, got_z), axis=1, keepdims=True)
    for i in range(NI):
        for j in range(NI):
            a = got[NI * NI + i:NI * NI + i + 1]
            b = got[NI * NI + j:NI * NI + j + 1]
            n = i * NI + j
            ray_ref[i:i + 1, j:j + 1] = got[n:n + 1] / jnp.sqrt(a * b)

    for c in range(T):
        for way in (1, -1):
            drain(pieces[c].at[pl.ds(0, X * (Y // 2 - 1) + X // 2)], send.at[group(("ring", c, way))])
        drain(pieces[c].at[pl.ds(0, X - 1)], send.at[group(("rx", c))])
    drain(vg.at[pl.ds(0, 24)], send.at[group("v")])
    drain(lg.at[pl.ds(0, 3 * T)], send.at[group("l")])
    drain(half, send.at[group("swap")])
    for h in range(H):
        drain(zgot.at[h, pl.ds(X, X * (Z - 1))], send.at[group(("z", h))])
        drain(fgot.at[h, pl.ds(0, X - 1)], send.at[group(("f", h))])
    for buf, size, name in ((gk, C, "dk"), (gx, X, "dx"), (gy, Y, "dy"), (gz, Z, "dz")):
        drain(buf.at[pl.ds(0, size - 1)], send.at[group(name)])
    assert len(used) <= recv.shape[0] and len(groups) <= send.shape[0], (len(used), len(groups))


def local(Y, Z, vectors, left_ops, right_ops, offsets):
    NI, _, PP, B, _ = vectors.shape
    T = left_ops.shape[0]
    Q, ZC = B // X, Z * C
    R, HQ = B // ZC, Q // H
    bf, f32 = jnp.bfloat16, jnp.float32
    vmem, dma = pltpu.VMEM, pltpu.SemaphoreType.DMA
    W = PP * HQ
    whole = pl.BlockSpec(memory_space=pltpu.VMEM)
    hbm = pl.BlockSpec(memory_space=pl.ANY)
    products, rayleigh = pl.pallas_call(
        functools.partial(kernel, Y, Z),
        out_shape=(jax.ShapeDtypeStruct((NI, PP, R, B), bf), jax.ShapeDtypeStruct((NI, NI), f32)),
        in_specs=[pl.BlockSpec(memory_space=pltpu.SMEM), hbm, hbm, hbm],
        out_specs=(whole, whole),
        scratch_shapes=[
            vmem((NI, PP, B, B), bf),
            vmem((T, B, B), bf),
            vmem((T, B, B), bf),
            vmem((X, T, Q, B), bf),
            vmem((Y * X, Q, B), bf),
            vmem((Y * X, Q, B), bf),
            vmem((Y * X, Q, B), bf),
            vmem((X * T, B, B), bf),
            vmem((X * NI * PP, B, B), bf),
            vmem((X, T, PP, NI * B, B), bf),
            vmem((H, X, NI, ZC, R, W), f32),
            vmem((H, X, NI, ZC, R, W), bf),
            vmem((H, X, NI, Z, R, W), bf),
            vmem((H, X, NI, Z, R, W), bf),
            vmem((H, X, Z, NI, R, W), bf),
            vmem((H, X * Z, NI, R, W), bf),
            vmem((H, X, NI, R, W), bf),
            vmem((H, X, NI, R, W), bf),
            vmem((X, 8, W), f32),
            vmem((C, 8, W), f32),
            vmem((Z, 8, W), f32),
            vmem((Y, 8, W), f32),
            dma((3,)),
            dma((GROUPS,)),
            dma((ARRIVALS,)),
        ],
        compiler_params=pltpu.CompilerParams(
            collective_id=0, has_side_effects=True, vmem_limit_bytes=56 * 1024 * 1024),
    )(offsets, vectors[:, 0], left_ops[:, 0], right_ops[:, 0])
    return products[:, None], rayleigh


def solution(mesh):
    sectors, terms = mesh.shape["sec"], mesh.shape["term"]
    in_specs = (
        P(None, "sec", None, None, None),
        P("term", "sec", None, None),
        P("term", "sec", None, None),
        P("term", None),
    )
    out_specs = (P(None, "sec", None, "term", None), P())
    return jax.shard_map(
        functools.partial(local, sectors // X, terms // C),
        mesh=mesh, in_specs=in_specs, out_specs=out_specs, check_vma=False)
```

```python
import functools

import jax
import jax.numpy as jnp
from jax import lax
from jax.experimental import pallas as pl
from jax.experimental.pallas import tpu as pltpu
from jax.sharding import PartitionSpec as P

MESH = pl.DeviceIdType.MESH
X = 4
C = 2
H = 1
ORDER = (0, 3, 1, 2)
GROUPS = 18
ARRIVALS = 95


def kernel(Y, Z, off_ref, v_hbm, l_hbm, r_hbm, prod_ref, ray_ref,
           v_ref, l_ref, r_ref, rt, g0, g1, g2, lg, vg, inner, part, vcol, half, other,
           zsend, zgot, fin, fgot, gx, gk, gz, gy, load, send, recv):
    NI, PP, B, _ = v_ref.shape
    T = l_ref.shape[0]
    Q = B // X
    HQ = Q // H
    ZC = Z * C
    R = B // ZC
    PH = PP // C
    sec, term = lax.axis_index("sec"), lax.axis_index("term")
    x, y = sec // Y, sec % Y
    z, k = term // C, term % C
    w = z % 2
    f32, bf = jnp.float32, jnp.bfloat16

    def at(dx=0, dy=0, dz=0, dk=0):
        return (((x + dx) % X) * Y + (y + dy) % Y, ((z + dz) % Z) * C + (k + dk) % C)

    loads = [pltpu.make_async_copy(a, b, load.at[n]) for n, (a, b) in enumerate(
        ((r_hbm, r_ref), (v_hbm, v_ref), (l_hbm, l_ref)))]
    for made in loads:
        made.start()
    barrier = pltpu.get_barrier_semaphore()
    peers = [at(dx=d) for d in range(1, X)] + [at(dy=d) for d in range(1, Y)]
    peers += [at(dz=d) for d in range(1, Z)] + [at(dk=1)]
    for peer in peers:
        pl.semaphore_signal(barrier, inc=1, device_id=peer, device_id_type=MESH)
    loads[0].wait()
    for t in range(T):
        turned = r_ref[t].T
        for q in range(X):
            rt[q, t] = turned[q * Q:(q + 1) * Q]
    pieces = (g0, g1, g2)
    where = tuple((t, pl.ds(0, Q)) for t in range(T))
    for c, (t, rows) in enumerate(where):
        pieces[c][0] = rt[x, t, rows]
    loads[1].wait()
    loads[2].wait()
    pl.semaphore_wait(barrier, len(peers))

    used = []
    groups = {}

    def group(name):
        return groups.setdefault(name, len(groups))

    def fresh():
        used.append(0)
        return recv.at[len(used) - 1]

    def copy(src, dst, to, sent, got=None):
        made = pltpu.make_async_remote_copy(
            src_ref=src, dst_ref=dst, send_sem=send.at[group(sent)],
            recv_sem=fresh() if got is None else got,
            device_id=to, device_id_type=MESH)
        made.start()
        return made

    def drain(ref, sem):
        pltpu.make_async_copy(ref, ref, sem).wait()

    ring = {}

    def ring_send(c, d, first, count):
        g = pieces[c]
        for way in (1, -1):
            if 2 * d == Y and (first < X // 2) != (way == 1):
                continue
            ring[c, d, way, first, count] = copy(
                g.at[pl.ds(((-way * (d - 1)) % Y) * X + first, count)],
                g.at[pl.ds(((-way * d) % Y) * X + first, count)], at(dy=way), ("ring", c, way))

    def ring_pass(c, d):
        if 2 * d > Y:
            return
        for first in (0, 2):
            for key, made in list(ring.items()):
                if key[:2] == (c, d) and first <= key[3] < first + 2:
                    made.wait_recv()
            if 2 * d < Y:
                ring_send(c, d + 1, first, 2)

    rx = {}
    for c, (t, rows) in enumerate(where):
        got = None if c == 0 else fresh()
        for d in (1, 3, 2):
            rx[c, d] = copy(
                rt.at[(x + d) % X, t, rows], pieces[c].at[(-d) % X], at(dx=d), ("rx", c), got)
        rx[c] = got
        ring_send(c, 1, 0, 1)

    vx, vfwd, vz, vk, lx, lfwd = {}, {}, {}, {}, {}, {}

    def v_at(slot, i, n, core=k):
        return vg.at[(slot * NI + i) * PP + core * PH + n]

    for first in (0, 1):
        for way in (1, -1):
            n = first if way == 1 else 1 - first
            vx[way, n] = copy(v_ref.at[w, k * PH + n], v_at((-way) % X, w, n), at(dx=way), "v")

    def left_send(t):
        for way in (1, -1):
            lx[way, t] = copy(l_ref.at[t], lg.at[((-way) % X) * T + t], at(dx=way), "l")

    def left_pass(t):
        hb = B // 2
        for way in (1, -1):
            lx[way, t].wait_recv()
            rows = pl.ds(0 if way == 1 else hb, hb)
            lfwd[way, t] = copy(lg.at[((-way) % X) * T + t, rows], lg.at[2 * T + t, rows], at(dx=way), "l")

    def v_core_copy(slot, i, m, n):
        if (slot, m) not in vk:
            vk[slot, m] = fresh()
        copy(v_at(slot, i, n), v_at(slot, i, n), at(dk=1), "v", vk[slot, m])

    def v_share(slot, n):
        vz[slot, n] = copy(v_at(slot, w, n), v_at(slot, w, n), at(dz=-1 if n == 0 else 1), "v")
        v_core_copy(slot, w, 0, n)

    def v_pass(way, n):
        vx[way, n].wait_recv()
        slot = (-way) % X
        if (way, n) in ((1, 0), (-1, 1)):
            vfwd[n] = copy(v_at(slot, w, n), v_at(2, w, n), at(dx=way), "v")
        v_share(slot, n)

    def v_core(slot, n):
        vz[slot, n].wait_recv()
        v_core_copy(slot, 1 - w, 1, n)

    def v_wait(slot):
        for m in range(2):
            drain(vg.at[pl.ds(slot * NI * PP, PH)], vk[slot, m])

    def make_inner(o, t):
        d = ORDER[o]

        def body(p, carry):
            left = l_ref[t] if d == 0 else lg[d * T + t]
            for i in range(NI):
                v = v_ref[i, p] if d == 0 else vg[(d * NI + i) * PP + p]
                inner[o, t, p, i * B:(i + 1) * B] = jnp.dot(
                    left, v, preferred_element_type=f32).astype(bf)
            return carry

        lax.fori_loop(0, PP, body, 0)

    def make_columns(o):
        d = ORDER[o]
        for q in range(X):
            @pl.when(x == q)
            def _():
                def body(i, carry):
                    for p in range(PP):
                        for h in range(H):
                            cols = slice(q * Q + h * HQ, q * Q + (h + 1) * HQ)
                            v = v_ref[i, p, :, cols] if d == 0 else vg[(d * NI + i) * PP + p, :, cols]
                            vcol[h, o, i, :, :, p * HQ:(p + 1) * HQ] = v.reshape(ZC, R, HQ)
                    return carry

                lax.fori_loop(0, NI, body, 0)

    def outer(c, o):
        d = ORDER[o]
        t = where[c][0]
        for p in range(PP):
            off = off_ref[t, p]
            dy = off % Y
            dx = (d + off // Y + jnp.where(y + dy >= Y, 1, 0)) % X
            total = lax.dot_general(
                inner[o, t, p], pieces[c][dy * X + dx], (((1,), (1,)), ((), ())),
                preferred_element_type=f32)
            cols = slice(p * HQ, (p + 1) * HQ)
            for h in range(H):
                here = total[:, h * HQ:(h + 1) * HQ].reshape(NI, ZC, R, HQ)
                if c == 0:
                    part[h, o, :, :, :, cols] = here
                else:
                    part[h, o, :, :, :, cols] += here

    swap = {}
    zsem = [fresh() for h in range(H)]
    fsem = [fresh() for h in range(H)]

    def swap_send(h, o):
        for i in range(NI):
            for n in range(Z):
                half[h, o, i, n] = part[h, o, i, n * C + 1 - k].astype(bf)
        swap[h, o] = copy(half.at[h, o], other.at[h, o], at(dk=1), "swap")

    def swap_add(h, o):
        swap[h, o].wait_recv()
        for i in range(NI):
            for n in range(Z):
                total = part[h, o, i, n * C + k] + other[h, o, i, n].astype(f32)
                zsend[h, o, n, i] = total.astype(bf)
        for dz in sorted(range(1, Z), key=lambda d: -min(d, Z - d)):
            copy(zsend.at[h, o, (z + dz) % Z], zgot.at[h, ((-dz) % Z) * X + o], at(dz=dz), ("z", h), zsem[h])

    def gram_add(h, o, carry):
        def body(n, carry):
            out = list(carry)
            for i in range(NI):
                v = vcol[h, o, i, n].astype(f32)
                for j in range(NI):
                    out[i * NI + j] = out[i * NI + j] + v * part[h, o, j, n]
            return tuple(out)

        return lax.fori_loop(0, ZC, body, carry)

    def finish(h):
        drain(zgot.at[h, pl.ds(X, X * (Z - 1))], zsem[h])
        for o in range(X):
            for i in range(NI):
                total = zsend[h, o, z, i].astype(f32)
                for dz in range(1, Z):
                    total = total + zgot[h, dz * X + o, i].astype(f32)
                fin[h, o, i] = total.astype(bf)
            if o:
                copy(fin.at[h, o], fgot.at[h, x], at(dx=ORDER[o]), ("f", h), fsem[h])
        fgot[h, x] = fin[h, 0]

    def spread(buf, me, size, name):
        got = fresh()
        for d in range(1, size):
            copy(buf.at[me], buf.at[me], at(**{name: d}), name, got)
        return got

    def collect(buf, size, got):
        drain(buf.at[pl.ds(0, size - 1)], got)
        return jnp.sum(buf[...], axis=0)

    left_send(0)
    make_inner(0, 0)
    for d in (1, 3, 2):
        rx[0, d].wait_recv()
        ring_send(0, 1, (-d) % X, 1)
    make_inner(0, 1)
    for c in range(1, T):
        drain(pieces[c].at[pl.ds(1, X - 1)], rx[c])
        ring_send(c, 1, 1, 1)
        ring_send(c, 1, 2, 2)
    make_inner(0, 2)
    ring_pass(0, 1)
    v_pass(1, 0)
    v_pass(-1, 1)
    left_send(1)
    left_send(2)
    ring_pass(1, 1)
    make_columns(0)
    v_pass(1, 1)
    v_pass(-1, 0)
    ring_pass(0, 2)

    def squares(n, carry):
        rows = pl.ds(pl.multiple_of(n * 16, 16), 16)
        out = []
        for i in range(NI):
            total = carry[i]
            for p in range(PP):
                v = v_ref[i, p, rows].astype(f32)
                total = total + v * v
            out.append(total)
        return tuple(out)

    square = lax.fori_loop(0, B // 16, squares, (jnp.zeros((16, B), f32),) * NI)
    left_pass(0)
    ring_pass(1, 2)
    ring_pass(2, 1)
    for slot in (3, 1):
        v_core(slot, 0)
        v_core(slot, 1)
    v_wait(3)
    make_inner(1, 0)
    ring_pass(0, 3)
    for n in range(PH):
        vfwd[n].wait_recv()
        v_share(2, n)
    left_pass(1)
    make_inner(1, 1)
    ring_pass(1, 3)
    left_pass(2)
    make_inner(1, 2)
    ring_pass(2, 2)
    v_wait(1)
    make_inner(2, 0)
    v_core(2, 0)
    v_core(2, 1)
    make_inner(2, 1)
    ring_pass(0, 4)
    make_inner(2, 2)
    outer(0, 0)
    outer(0, 1)
    outer(0, 2)
    ring_pass(2, 3)
    ring_pass(1, 4)
    outer(1, 0)
    outer(1, 1)
    outer(1, 2)
    v_wait(2)
    for t in range(T):
        for way in (1, -1):
            lfwd[way, t].wait_recv()
        make_inner(3, t)
    outer(0, 3)
    outer(1, 3)
    ring_pass(2, 4)
    for o in range(X):
        outer(2, o)
        swap_send(0, o)
        if o > 1:
            swap_add(0, o - 2)
    swap_add(0, 2)
    swap_add(0, 3)
    for o in range(1, X):
        make_columns(o)
    gram = (jnp.zeros((R, PP * HQ), f32),) * (NI * NI)
    for h in range(H):
        for o in range(X):
            gram = gram_add(h, o, gram)

    rows = [jnp.sum(g, axis=0, keepdims=True) for g in gram]
    W = rows[0].shape[1]
    for s in square:
        s = jnp.sum(s, axis=0, keepdims=True) * (1.0 / ZC)
        rows.append(sum(s[:, n * W:(n + 1) * W] for n in range(1, B // W)) + s[:, :W])
    for n in range(8):
        gk[k, n:n + 1] = rows[n] if n < len(rows) else jnp.zeros_like(rows[0])
    got_k = spread(gk, k, C, "dk")
    gx[x] = collect(gk, C, got_k)
    got_x = spread(gx, x, X, "dx")
    gy[y] = collect(gx, X, got_x)
    got_y = spread(gy, y, Y, "dy")
    gz[z] = collect(gy, Y, got_y)
    got_z = spread(gz, z, Z, "dz")
    finish(0)
    for h in range(H):
        drain(fgot.at[h, pl.ds(0, X - 1)], fsem[h])
    for q in range(X):
        for i in range(NI):
            for p in range(PP):
                prod_ref[i, p, :, q * Q:(q + 1) * Q] = jnp.concatenate(
                    [fgot[h, q, i, :, p * HQ:(p + 1) * HQ] for h in range(H)], axis=1)
    got = jnp.sum(collect(gz, Z, got_z), axis=1, keepdims=True)
    for i in range(NI):
        for j in range(NI):
            a = got[NI * NI + i:NI * NI + i + 1]
            b = got[NI * NI + j:NI * NI + j + 1]
            n = i * NI + j
            ray_ref[i:i + 1, j:j + 1] = got[n:n + 1] / jnp.sqrt(a * b)

    for c in range(T):
        for way in (1, -1):
            drain(pieces[c].at[pl.ds(0, X * (Y // 2 - 1) + X // 2)], send.at[group(("ring", c, way))])
        drain(pieces[c].at[pl.ds(0, X - 1)], send.at[group(("rx", c))])
    drain(vg.at[pl.ds(0, 24)], send.at[group("v")])
    drain(lg.at[pl.ds(0, 3 * T)], send.at[group("l")])
    drain(half, send.at[group("swap")])
    for h in range(H):
        drain(zgot.at[h, pl.ds(X, X * (Z - 1))], send.at[group(("z", h))])
        drain(fgot.at[h, pl.ds(0, X - 1)], send.at[group(("f", h))])
    for buf, size, name in ((gk, C, "dk"), (gx, X, "dx"), (gy, Y, "dy"), (gz, Z, "dz")):
        drain(buf.at[pl.ds(0, size - 1)], send.at[group(name)])
    assert len(used) <= recv.shape[0] and len(groups) <= send.shape[0], (len(used), len(groups))


def local(Y, Z, vectors, left_ops, right_ops, offsets):
    NI, _, PP, B, _ = vectors.shape
    T = left_ops.shape[0]
    Q, ZC = B // X, Z * C
    R, HQ = B // ZC, Q // H
    bf, f32 = jnp.bfloat16, jnp.float32
    vmem, dma = pltpu.VMEM, pltpu.SemaphoreType.DMA
    W = PP * HQ
    whole = pl.BlockSpec(memory_space=pltpu.VMEM)
    hbm = pl.BlockSpec(memory_space=pl.ANY)
    products, rayleigh = pl.pallas_call(
        functools.partial(kernel, Y, Z),
        out_shape=(jax.ShapeDtypeStruct((NI, PP, R, B), bf), jax.ShapeDtypeStruct((NI, NI), f32)),
        in_specs=[pl.BlockSpec(memory_space=pltpu.SMEM), hbm, hbm, hbm],
        out_specs=(whole, whole),
        scratch_shapes=[
            vmem((NI, PP, B, B), bf),
            vmem((T, B, B), bf),
            vmem((T, B, B), bf),
            vmem((X, T, Q, B), bf),
            vmem((Y * X, Q, B), bf),
            vmem((Y * X, Q, B), bf),
            vmem((Y * X, Q, B), bf),
            vmem((X * T, B, B), bf),
            vmem((X * NI * PP, B, B), bf),
            vmem((X, T, PP, NI * B, B), bf),
            vmem((H, X, NI, ZC, R, W), f32),
            vmem((H, X, NI, ZC, R, W), bf),
            vmem((H, X, NI, Z, R, W), bf),
            vmem((H, X, NI, Z, R, W), bf),
            vmem((H, X, Z, NI, R, W), bf),
            vmem((H, X * Z, NI, R, W), bf),
            vmem((H, X, NI, R, W), bf),
            vmem((H, X, NI, R, W), bf),
            vmem((X, 8, W), f32),
            vmem((C, 8, W), f32),
            vmem((Z, 8, W), f32),
            vmem((Y, 8, W), f32),
            dma((3,)),
            dma((GROUPS,)),
            dma((ARRIVALS,)),
        ],
        compiler_params=pltpu.CompilerParams(
            collective_id=0, has_side_effects=True, vmem_limit_bytes=56 * 1024 * 1024),
    )(offsets, vectors[:, 0], left_ops[:, 0], right_ops[:, 0])
    return products[:, None], rayleigh


def solution(mesh):
    sectors, terms = mesh.shape["sec"], mesh.shape["term"]
    in_specs = (
        P(None, "sec", None, None, None),
        P("term", "sec", None, None),
        P("term", "sec", None, None),
        P("term", None),
    )
    out_specs = (P(None, "sec", None, "term", None), P())
    return jax.shard_map(
        functools.partial(local, sectors // X, terms // C),
        mesh=mesh, in_specs=in_specs, out_specs=out_specs, check_vma=False)
```
